32 devices in a mesh: dp: 8 (over y, x, core), tensor: 4 (over z).
Axes of the slice: x: 2, y: 2, z: 4, core: 2. Of those that a mesh axis runs over, the one named last changes fastest.
Arguments:
- points: bfloat16 [8192, 256], P('dp'), as said below
- centers: bfloat16 [32768, 256], P(('dp', 'tensor')), as said below
- factors: bfloat16 [32768, 32768], P('tensor', 'dp'), may hold values from -0.015625 to 0.015625
- column_scale: float32 [32768], P(('dp', 'tensor')), may hold values from 80 to 320
- iterate: float32 [64, 32768], P(None, ('dp', 'tensor')), may hold values from -6 to 6
- residual: float32 [64, 32768], P(None, ('dp', 'tensor')), may hold values from -6 to 6
- direction: float32 [64, 32768], P(None, ('dp', 'tensor')), may hold values from -6 to 6
Outputs:
- new_iterate: float32 [64, 32768], P(None, ('dp', 'tensor'))
- new_residual: float32 [64, 32768], P(None, ('dp', 'tensor'))
- new_direction: float32 [64, 32768], P(None, ('dp', 'tensor'))
The draws below stay inside these ranges and needn't reach their ends.
Inputs may be any that keep to these rules, and one draw needn't show every extreme that they name: `points`: real embeddings of any row scale. `centers`: real embeddings of any row scale.
All inputs are finite; a program needn't handle non-finite values.
Results may differ from the reference program's by a relative error of at most 0.0058.
The reference program's roundings to bfloat16 on the way count: a program that leaves them out, or rounds other values in their place, can miss the bound.
Values may be sent and summed in bfloat16 or wider, within the bound.
A program may use at most 448 MiB of HBM per device.

```python
import math
import jax
import jax.numpy as jnp
from jax import lax

D = 256
M = 32768
R = 64
PTS_DEV = 1024
N = 8192
N_DP = 8
N_TENSOR = 4


def draw_rows(key, row_count, label):
    clusters = max(min(M, N) // 16, 4)
    mean_key = jax.random.fold_in(key, 7)
    base_key = jax.random.fold_in(key, label)
    members = jax.random.randint(jax.random.fold_in(base_key, 5), (row_count,), 0, clusters)
    cluster_means = jax.random.normal(mean_key, (clusters, D), jnp.float32)
    jitter = jax.random.normal(jax.random.fold_in(base_key, 1), (row_count, D), jnp.float32)
    spread = jnp.exp(jax.random.uniform(jax.random.fold_in(base_key, 3), (row_count, 1), jnp.float32, math.log(0.15), math.log(0.6)))
    row_scale = jnp.exp(jax.random.uniform(jax.random.fold_in(base_key, 2), (row_count, 1), jnp.float32, 0.0, math.log(10.0)))
    values = (jnp.take(cluster_means, members, axis=0) + spread * jitter) * row_scale
    return values.astype(jnp.bfloat16)


def draw_points(key, part):
    return draw_rows(key, N, 3)


def draw_centers(key, part):
    return draw_rows(key, M, 4)


def steps_of(own_key, dims, cuts, low, top_value):
    factor_of, own = 1.0, jax.random.fold_in(own_key, 6)
    for position, shards_of in cuts:
        draws = jnp.exp(jax.random.uniform(jax.random.fold_in(own, position), (shards_of,), jnp.float32, low / len(cuts), top_value / len(cuts)))
        factor_of = factor_of * jnp.repeat(draws, dims[position] // shards_of).reshape([-1 if axis == position else 1 for axis in range(len(dims))])
    return factor_of


def centred(stream_key, shape, scale, bound, split=(), kind=jnp.bfloat16):
    values = jax.random.normal(stream_key, shape, jnp.float32) * scale
    if len(split) > 0:
        values = steps_of(stream_key, shape, split, -0.22, 0.18) * values
    return jnp.clip(values, min=-bound, max=bound).astype(kind)


def setup_inputs(seed: int = 0) -> dict:
    key_of = jax.random.split(jax.random.key(seed), 8)
    return {
        "points": draw_points(jax.random.fold_in(key_of[7], 71), 0),
        "centers": draw_centers(jax.random.fold_in(key_of[7], 71), 0),
        "factors": centred(key_of[2], (M, M), (4 * M) ** -0.5, 0.015625, ((0, 4), (1, 8))),
        "column_scale": jnp.clip(jnp.exp(math.log(320.0) - 1.3862944 * jax.random.uniform(key_of[3], (M,), jnp.float32) ** steps_of(key_of[3], (M,), ((0, 32),), -0.2, 0.2)), 80.0, 320.0),
        "iterate": centred(key_of[4], (R, M), 1.0, 6.0, ((1, 32),), jnp.float32),
        "residual": centred(key_of[5], (R, M), 1.0, 6.0, ((1, 32),), jnp.float32),
        "direction": centred(key_of[6], (R, M), 1.0, 6.0, ((1, 32),), jnp.float32),
    }


kernel_gamma = 8.0
ridge_penalty = 0.0001

def normalized(rows):
    widened = rows.astype(jnp.float32)
    inv_rms = lax.rsqrt(lax.optimization_barrier(jnp.mean(widened * widened, axis=1, keepdims=True)) + 1e-06)
    return (widened * inv_rms).astype(jnp.bfloat16)

def masked_block(block, offset, upper_part):
    block_rows, row_width = block.shape
    row_ids = offset + lax.broadcasted_iota(jnp.int32, (block_rows, row_width), 0)
    col_ids = lax.broadcasted_iota(jnp.int32, (block_rows, row_width), 1)
    keep_mask = col_ids >= row_ids if upper_part else col_ids < row_ids
    return jnp.where(keep_mask, block, jnp.zeros_like(block))

def left_mul(vector, blocks, upper_part):
    block_count, block_rows, row_width = blocks.shape
    offsets = jnp.arange(block_count, dtype=jnp.int32) * block_rows

    def advance(total, element):
        block, offset = element
        masked = masked_block(block, offset, upper_part)
        segment = lax.dynamic_slice_in_dim(vector, offset, block_rows, 1)
        return (total + jnp.dot(segment, masked, preferred_element_type=jnp.float32), None)
    total, unused = lax.scan(advance, jnp.zeros((vector.shape[0], row_width), jnp.float32), (blocks, offsets))
    return total

def right_mul(vector, blocks, upper_part):
    block_count, block_rows, row_width = blocks.shape
    offsets = jnp.arange(block_count, dtype=jnp.int32) * block_rows

    def advance(carry, element):
        block, offset = element
        masked = masked_block(block, offset, upper_part)
        result = lax.dot_general(vector, masked, (((1,), (1,)), ((), ())), preferred_element_type=jnp.float32)
        return (carry, result)
    unused, pieces = lax.scan(advance, jnp.zeros((), jnp.float32), (blocks, offsets))
    return pieces.transpose(1, 0, 2).reshape(vector.shape[0], block_count * block_rows)

def reference(points, centers, factors, column_scale, iterate, residual, direction):
    piece_len = M // (N_DP * N_TENSOR)
    ordered = factors.reshape(N_TENSOR, N_DP, piece_len, M).transpose(1, 0, 2, 3).reshape(M, M)
    blocks = ordered.reshape(16, M // 16, M)
    scale_row = column_scale[None, :]
    first = scale_row * (direction + left_mul(direction.astype(jnp.bfloat16), blocks, False))
    second = first + right_mul(first.astype(jnp.bfloat16), blocks, True)
    second_b = second.astype(jnp.bfloat16)
    center_rows = normalized(centers)
    point_blocks = points.reshape(N // PTS_DEV, PTS_DEV, D)

    def through_kernel(total, block):
        inner = jnp.dot(normalized(block), center_rows.T, preferred_element_type=jnp.float32)
        kernel = jnp.exp(kernel_gamma * (inner / D - 1.0)).astype(jnp.bfloat16)
        point_vals = lax.dot_general(second_b, kernel, (((1,), (1,)), ((), ())), preferred_element_type=jnp.float32)
        return (total + jnp.dot(point_vals.astype(jnp.bfloat16), kernel, preferred_element_type=jnp.float32), None)
    summed, unused = lax.scan(through_kernel, jnp.zeros((R, M), jnp.float32), point_blocks)
    back = summed / N
    third = back + left_mul(back.astype(jnp.bfloat16), blocks, True) + ridge_penalty * first
    weighted = scale_row * third
    image = weighted + right_mul(weighted.astype(jnp.bfloat16), blocks, False)
    old_norm = lax.optimization_barrier(jnp.sum(residual * residual, axis=1, keepdims=True))
    curvature = lax.optimization_barrier(jnp.sum(direction * image, axis=1, keepdims=True))
    step_size = old_norm / curvature
    new_iterate = iterate + step_size * direction
    new_residual = residual - step_size * image
    new_norm = lax.optimization_barrier(jnp.sum(new_residual * new_residual, axis=1, keepdims=True))
    new_direction = new_residual + new_norm / old_norm * direction
    return (new_iterate, new_residual, new_direction)
```

```python
import functools

import jax
import jax.numpy as jnp
from jax import lax
from jax.experimental import pallas as pl
from jax.experimental.pallas import tpu as pltpu
from jax.sharding import PartitionSpec as P

kernel_gamma = 8.0
ridge_penalty = 0.0001


def normalized(rows):
    widened = rows.astype(jnp.float32)
    inv_rms = lax.rsqrt(jnp.mean(widened * widened, axis=1, keepdims=True) + 1e-06)
    return (widened * inv_rms).astype(jnp.bfloat16)


def rows_in(vector_b):
    return lax.all_gather(vector_b, "dp", axis=1, tiled=True)


def cols_out(partial_value):
    return lax.psum_scatter(partial_value, "tensor", scatter_dimension=1, tiled=True)


def cols_in(vector_b):
    return lax.all_gather(vector_b, "tensor", axis=1, tiled=True)


def rows_out(partial_value):
    return lax.psum_scatter(partial_value, "dp", scatter_dimension=1, tiled=True)


def times_block(vector_rows, block):
    return jnp.dot(vector_rows, block, preferred_element_type=jnp.float32)


def times_block_t(vector_cols, block):
    return lax.dot_general(
        vector_cols, block, (((1,), (1,)), ((), ())), preferred_element_type=jnp.float32
    )


MESH = pl.DeviceIdType.MESH
SLOTS = 3
F32 = jnp.float32
BF16 = jnp.bfloat16


def dot_nn(a, b):
    return jnp.dot(a, b, preferred_element_type=F32)


def dot_nt(a, b):
    return lax.dot_general(a, b, (((1,), (1,)), ((), ())), preferred_element_type=F32)


def fused(
    nd,
    nt,
    points,
    centers,
    factors,
    scale,
    iterate,
    residual,
    direction,
    new_iterate,
    new_residual,
    new_direction,
    fbuf,
    kmat,
    xn,
    cen,
    rows,
    acc,
    own,
    first,
    zsend,
    zrecv,
    zgath,
    rsend,
    rrecv,
    psend,
    precv,
    pgath,
    stat_dp,
    stat_t,
    fsem,
    ag_s,
    ag_r,
    cag_s,
    cag_r,
    zr_s,
    zr_r,
    zg_s,
    zg_r,
    rs_s,
    rs_r,
    pr_s,
    pr_r,
    pg_s,
    pg_r,
    sd_s,
    sd_r,
    st_s,
    st_r,
):
    d = lax.axis_index("dp")
    t = lax.axis_index("tensor")
    piece = direction.shape[1]
    pts = points.shape[0]
    width = pts // nt
    core = lax.rem(d, 2)
    chip = lax.div(d, 2)
    nchip = nd // 2
    sib = d + 1 - 2 * core

    def dp_at(m):
        return lax.rem(d + m, nd)

    def t_at(m):
        return lax.rem(t + m, nt)

    def send(src, dst, ssem, rsem, dp, tp):
        return pltpu.make_async_remote_copy(
            src_ref=src,
            dst_ref=dst,
            send_sem=ssem,
            recv_sem=rsem,
            device_id=(dp, tp),
            device_id_type=MESH,
        )

    def load(q):
        slot = lax.rem(q, SLOTS)
        return pltpu.make_async_copy(
            factors.at[pl.ds(pl.multiple_of(q * piece, piece), piece), :],
            fbuf.at[slot],
            fsem.at[slot],
        )

    for q in range(SLOTS):
        load(jnp.int32(nd - 1 - q)).start()

    barrier = pltpu.get_barrier_semaphore()
    for m in range(1, nd):
        pl.semaphore_signal(barrier, inc=1, device_id=(dp_at(m), t), device_id_type=MESH)
    for m in range(1, nt):
        pl.semaphore_signal(barrier, inc=1, device_id=(d, t_at(m)), device_id_type=MESH)

    def normal(x):
        wide = x.astype(F32)
        inv = lax.rsqrt(jnp.mean(wide * wide, axis=1, keepdims=True) + 1e-06)
        return (wide * inv).astype(BF16)

    rows[0, d] = direction[...].astype(BF16)
    cen[d] = normal(centers[...])
    pl.semaphore_wait(barrier, nd - 1 + nt - 1)

    def out_copy(buf, ss, rs, m):
        if m == 0:
            return send(buf.at[d], buf.at[d], ss.at[0], rs.at[d], sib, t)
        to = lax.rem(chip + m, nchip) * 2 + core
        return send(buf.at[d], buf.at[d], ss.at[m], rs.at[d], to, t)

    def on_copy(buf, ss, rs, m):
        src = lax.rem(chip - m + nchip, nchip) * 2 + core
        return send(buf.at[src], buf.at[src], ss.at[nchip + m - 1], rs.at[src], sib, t)

    def ag_start(buf, ss, rs):
        for m in range(nchip):
            out_copy(buf, ss, rs, m).start()

    def ag_forward(buf, ss, rs):
        for m in range(1, nchip):
            c = on_copy(buf, ss, rs, m)
            c.wait_recv()
            c.start()

    def ag_finish(buf, ss, rs):
        for m in range(nchip):
            src = m * 2 + 1 - core
            send(buf.at[src], buf.at[src], ss.at[0], rs.at[src], sib, t).wait_recv()
        for m in range(nchip):
            out_copy(buf, ss, rs, m).wait_send()
        for m in range(1, nchip):
            on_copy(buf, ss, rs, m).wait_send()

    ag_start(rows.at[0], ag_s.at[0], ag_r.at[0])
    ag_start(cen, cag_s, cag_r)
    xn[...] = normal(points[...])
    ag_forward(rows.at[0], ag_s.at[0], ag_r.at[0])
    ag_finish(rows.at[0], ag_s.at[0], ag_r.at[0])

    def tile(q, j):
        return fbuf[lax.rem(q, SLOTS), :, pl.ds(pl.multiple_of(j * piece, piece), piece)]

    def masked(q, upper):
        block = tile(q, t)
        row = lax.broadcasted_iota(jnp.int32, (piece, piece), 0)
        col = lax.broadcasted_iota(jnp.int32, (piece, piece), 1)
        keep = col >= row if upper else col < row
        return jnp.where(keep, block, jnp.zeros_like(block))

    def times_rows(q, x, lo, hi):
        def step(j, carry):
            acc[j] += dot_nn(x, tile(q, j))
            return carry

        lax.fori_loop(lo, hi, step, 0)

    def times_cols(q, phase, lo, hi):
        def step(j, carry):
            own[...] += dot_nt(zgath[phase, j], tile(q, j))
            return carry

        lax.fori_loop(lo, hi, step, 0)

    def rs_copy(phase, q):
        return send(
            rsend.at[q], rrecv.at[phase, d], rs_s.at[phase, q], rs_r.at[phase, d], q, t
        )

    def rs_wait(phase, src):
        send(
            rsend.at[src], rrecv.at[phase, src], rs_s.at[phase, src], rs_r.at[phase, src], src, t
        ).wait_recv()

    def exchange(phase, finish):
        for m in range(1, nt):
            j = t_at(m)
            zsend[j] = acc[j].astype(BF16)
            send(
                zsend.at[j], zrecv.at[phase, t], zr_s.at[phase, j], zr_r.at[phase, t], d, j
            ).start()
        total = acc[t]
        for m in range(1, nt):
            j = t_at(m)
            send(
                zsend.at[j], zrecv.at[phase, j], zr_s.at[phase, j], zr_r.at[phase, j], d, j
            ).wait_recv()
            total = total + zrecv[phase, j].astype(F32)
        zgath[phase, t] = finish(total).astype(BF16)
        for m in range(1, nt):
            j = t_at(m)
            send(
                zgath.at[phase, t], zgath.at[phase, t], zg_s.at[phase, j], zg_r.at[phase, t], d, j
            ).start()
        for m in range(1, nt):
            j = t_at(m)
            send(
                zgath.at[phase, j], zgath.at[phase, j], zg_s.at[phase, j], zg_r.at[phase, j], d, j
            ).wait_recv()
        for m in range(1, nt):
            j = t_at(m)
            send(
                zsend.at[j], zrecv.at[phase, t], zr_s.at[phase, j], zr_r.at[phase, t], d, j
            ).wait_send()
            send(
                zgath.at[phase, t], zgath.at[phase, t], zg_s.at[phase, j], zg_r.at[phase, t], d, j
            ).wait_send()

    def factor_phase(phase, upper, finish):
        slab = rows.at[0 if phase == 0 else 2]
        down = not upper
        before = nd - 1 - d if down else d
        after = d if down else nd - 1 - d

        def nth(i):
            return nd - 1 - i if down else i

        def ready(i):
            if down:
                load(nth(i)).wait()
            else:

                @pl.when(i >= SLOTS)
                def _():
                    load(nth(i)).wait()

        def done(i):
            @pl.when(i + SLOTS < nd)
            def _():
                load(nth(i + SLOTS)).start()

        acc[...] = jnp.zeros_like(acc)

        def first_half(i, carry):
            ready(i)
            q = nth(i)
            times_rows(q, slab[q], 0, nt)
            done(i)
            return carry

        lax.fori_loop(0, before, first_half, 0)
        ready(before)
        x = slab[d]
        if upper:
            times_rows(d, x, t + 1, nt)
        else:
            times_rows(d, x, 0, t)
        acc[t] += dot_nn(x, masked(d, upper))
        exchange(phase, finish)

        def second_half(i, carry):
            ready(i)
            q = nth(i)
            own[...] = jnp.zeros_like(own)
            times_cols(q, phase, 0, nt)
            rsend[q] = own[...].astype(BF16)
            rs_copy(2 * phase, q).start()
            done(i)
            return carry

        own[...] = dot_nt(zgath[phase, t], masked(d, not upper))
        if upper:
            times_cols(d, phase, 0, t)
        else:
            times_cols(d, phase, t + 1, nt)
        done(before)
        kept = own[...]
        lax.fori_loop(before + 1, nd, second_half, 0)
        return kept

    def factor_sum(phase, upper, total):
        lo, hi = (0, d) if upper else (d + 1, nd)
        slo, shi = (d + 1, nd) if upper else (0, d)
        own[...] = total

        def got(src, carry):
            rs_wait(2 * phase, src)
            own[...] += rrecv[2 * phase, src].astype(F32)
            return carry

        lax.fori_loop(lo, hi, got, 0)

        def gone(q, carry):
            rs_copy(2 * phase, q).wait_send()
            return carry

        lax.fori_loop(slo, shi, gone, 0)
        return own[...]

    def form(lo, hi):
        def step(i, carry):
            q = lax.div(i, 4)
            at = pl.ds(pl.multiple_of(lax.rem(i, 4) * (pts // 4), pts // 4), pts // 4)
            inner = dot_nt(xn[at, :], cen[q])
            kmat[q, at, :] = jnp.exp(
                kernel_gamma * (inner / points.shape[1] - 1.0)
            ).astype(BF16)
            return carry

        lax.fori_loop(4 * lo, 4 * hi, step, 0)

    def finish_first(total):
        first[...] = scale[...] * (direction[...] + total)
        return first[...]

    kept = factor_phase(0, False, finish_first)
    ag_forward(cen, cag_s, cag_r)
    ag_finish(cen, cag_s, cag_r)
    acc[0] = kept
    form(0, nd // 2)
    second = factor_sum(0, False, first[...] + acc[0])
    rows[1, d] = second.astype(BF16)
    ag_start(rows.at[1], ag_s.at[1], ag_r.at[1])
    form(nd // 2, nd)
    ag_forward(rows.at[1], ag_s.at[1], ag_r.at[1])
    ag_finish(rows.at[1], ag_s.at[1], ag_r.at[1])

    own[:, :pts] = jnp.zeros((own.shape[0], pts), F32)

    def to_points(q, carry):
        own[:, :pts] += dot_nt(rows[1, q], kmat[q])
        return carry

    lax.fori_loop(0, nd, to_points, 0)
    for j in range(nt):
        acc[j, :, :width] = own[:, j * width : (j + 1) * width]
        psend[j] = own[:, j * width : (j + 1) * width].astype(BF16)
    for m in range(1, nt):
        j = t_at(m)
        send(psend.at[j], precv.at[t], pr_s.at[j], pr_r.at[t], d, j).start()
    total = acc[t, :, :width]
    for m in range(1, nt):
        j = t_at(m)
        send(psend.at[j], precv.at[j], pr_s.at[j], pr_r.at[j], d, j).wait_recv()
        total = total + precv[j].astype(F32)
    pgath[t] = total.astype(BF16)
    for m in range(1, nt):
        j = t_at(m)
        send(pgath.at[t], pgath.at[t], pg_s.at[j], pg_r.at[t], d, j).start()
    for m in range(1, nt):
        j = t_at(m)
        send(pgath.at[j], pgath.at[j], pg_s.at[j], pg_r.at[j], d, j).wait_recv()
    for m in range(1, nt):
        j = t_at(m)
        send(psend.at[j], precv.at[t], pr_s.at[j], pr_r.at[t], d, j).wait_send()
        send(pgath.at[t], pgath.at[t], pg_s.at[j], pg_r.at[t], d, j).wait_send()

    def from_points(q):
        part = dot_nn(pgath[0], kmat[q, :width, :])
        for j in range(1, nt):
            part += dot_nn(pgath[j], kmat[q, j * width : (j + 1) * width, :])
        return part / (pts * nd)

    def back_step(m, carry):
        q = lax.rem(d + m, nd)
        rsend[q] = from_points(q).astype(BF16)
        rs_copy(1, q).start()
        return carry

    lax.fori_loop(1, nd, back_step, 0)
    own[...] = from_points(d)

    def back_sum(m, carry):
        src = lax.rem(d + nd - m, nd)
        rs_wait(1, src)
        own[...] += rrecv[1, src].astype(F32)
        return carry

    lax.fori_loop(1, nd, back_sum, 0)

    def back_gone(m, carry):
        rs_copy(1, lax.rem(d + m, nd)).wait_send()
        return carry

    lax.fori_loop(1, nd, back_gone, 0)
    back = own[...]
    rows[2, d] = back.astype(BF16)
    ag_start(rows.at[2], ag_s.at[2], ag_r.at[2])
    first[...] = back + ridge_penalty * first[...]
    ag_forward(rows.at[2], ag_s.at[2], ag_r.at[2])
    ag_finish(rows.at[2], ag_s.at[2], ag_r.at[2])

    def finish_weighted(total):
        first[...] = scale[...] * (first[...] + total)
        return first[...]

    kept = factor_phase(1, True, finish_weighted)
    image = factor_sum(1, True, first[...] + kept)
    r = residual[...]
    p = direction[...]
    lane = lax.broadcasted_iota(jnp.int32, (r.shape[0], 128), 1)

    def summed(v):
        return jnp.sum(v, axis=1, keepdims=True)

    stat = jnp.where(lane == 0, summed(r * r), 0.0)
    stat = jnp.where(lane == 1, summed(p * image), stat)
    stat = jnp.where(lane == 2, summed(r * image), stat)
    stat = jnp.where(lane == 3, summed(image * image), stat)
    stat_dp[d] = stat

    def stat_copy(m):
        q = dp_at(m)
        return send(stat_dp.at[d], stat_dp.at[d], sd_s.at[q], sd_r.at[d], q, t)

    for m in range(1, nd):
        stat_copy(m).start()
    for m in range(1, nd):
        q = dp_at(m)
        send(stat_dp.at[q], stat_dp.at[q], sd_s.at[q], sd_r.at[q], q, t).wait_recv()
    stat = stat_dp[0]
    for q in range(1, nd):
        stat = stat + stat_dp[q]
    stat_t[t] = stat
    for m in range(1, nt):
        j = t_at(m)
        send(stat_t.at[t], stat_t.at[t], st_s.at[j], st_r.at[t], d, j).start()
    for m in range(1, nt):
        j = t_at(m)
        send(stat_t.at[j], stat_t.at[j], st_s.at[j], st_r.at[j], d, j).wait_recv()
    for m in range(1, nt):
        j = t_at(m)
        send(stat_t.at[t], stat_t.at[t], st_s.at[j], st_r.at[t], d, j).wait_send()
    for m in range(1, nd):
        stat_copy(m).wait_send()
    stat = stat_t[0]
    for j in range(1, nt):
        stat = stat + stat_t[j]
    old_norm, curvature = stat[:, 0:1], stat[:, 1:2]
    cross, image_norm = stat[:, 2:3], stat[:, 3:4]
    step_size = old_norm / curvature
    new_iterate[...] = iterate[...] + step_size * p
    image = own[...]
    nr = r - step_size * image
    new_residual[...] = nr
    new_norm = old_norm - 2.0 * step_size * cross + step_size * step_size * image_norm
    new_direction[...] = nr + new_norm / old_norm * p


def fused_shards(nd, nt, points, centers, factors, column_scale, iterate, residual, direction):
    r, piece = direction.shape
    pts, dim = points.shape
    local_cols = factors.shape[1]
    width = pts // nt
    vmem = pl.BlockSpec(memory_space=pltpu.VMEM)
    dma = pltpu.SemaphoreType.DMA
    return pl.pallas_call(
        functools.partial(fused, nd, nt),
        out_shape=(jax.ShapeDtypeStruct((r, piece), F32),) * 3,
        in_specs=[vmem, vmem, pl.BlockSpec(memory_space=pl.ANY), vmem, vmem, vmem, vmem],
        out_specs=(vmem, vmem, vmem),
        scratch_shapes=[
            pltpu.VMEM((SLOTS, piece, local_cols), BF16),
            pltpu.VMEM((nd, pts, piece), BF16),
            pltpu.VMEM((pts, dim), BF16),
            pltpu.VMEM((nd, piece, dim), BF16),
            pltpu.VMEM((3, nd, r, piece), BF16),
            pltpu.VMEM((nt, r, piece), F32),
            pltpu.VMEM((r, piece), F32),
            pltpu.VMEM((r, piece), F32),
            pltpu.VMEM((nt, r, piece), BF16),
            pltpu.VMEM((2, nt, r, piece), BF16),
            pltpu.VMEM((2, nt, r, piece), BF16),
            pltpu.VMEM((nd, r, piece), BF16),
            pltpu.VMEM((3, nd, r, piece), BF16),
            pltpu.VMEM((nt, r, width), BF16),
            pltpu.VMEM((nt, r, width), BF16),
            pltpu.VMEM((nt, r, width), BF16),
            pltpu.VMEM((nd, r, 128), F32),
            pltpu.VMEM((nt, r, 128), F32),
            dma((SLOTS,)),
            dma((3, nd)),
            dma((3, nd)),
            dma((nd,)),
            dma((nd,)),
            dma((2, nt)),
            dma((2, nt)),
            dma((2, nt)),
            dma((2, nt)),
            dma((3, nd)),
            dma((3, nd)),
            dma((nt,)),
            dma((nt,)),
            dma((nt,)),
            dma((nt,)),
            dma((nd,)),
            dma((nd,)),
            dma((nt,)),
            dma((nt,)),
        ],
        compiler_params=pltpu.CompilerParams(
            collective_id=0, has_side_effects=True, vmem_limit_bytes=63 * 1024 * 1024
        ),
    )(points, centers, factors, column_scale[None, :], iterate, residual, direction)


def shards(points, centers, factors, column_scale, iterate, residual, direction):
    piece_len = iterate.shape[1]
    local_rows, local_cols = factors.shape
    dp_index = lax.axis_index("dp")
    tensor_index = lax.axis_index("tensor")
    tensor_count = lax.axis_size("tensor")
    total_points = points.shape[0] * lax.axis_size("dp")
    row_pos = lax.broadcasted_iota(jnp.int32, (local_rows, local_cols), 0)
    row_ids = (row_pos // piece_len * tensor_count + tensor_index) * piece_len + row_pos % piece_len
    col_ids = dp_index * local_cols + lax.broadcasted_iota(jnp.int32, (local_rows, local_cols), 1)
    zero_block = jnp.zeros_like(factors)
    lower = jnp.where(col_ids < row_ids, factors, zero_block)
    upper = jnp.where(col_ids >= row_ids, factors, zero_block)
    scale_row = column_scale[None, :]
    first = scale_row * (
        direction + cols_out(times_block(rows_in(direction.astype(jnp.bfloat16)), lower))
    )
    second = first + rows_out(times_block_t(cols_in(first.astype(jnp.bfloat16)), upper))
    second_rows = rows_in(second.astype(jnp.bfloat16))
    center_rows = lax.all_gather(normalized(centers), "dp", axis=0, tiled=True)
    inner = jnp.dot(normalized(points), center_rows.T, preferred_element_type=jnp.float32)
    kernel = jnp.exp(kernel_gamma * (inner / points.shape[1] - 1.0)).astype(jnp.bfloat16)
    point_part = times_block_t(second_rows, kernel)
    point_vals = lax.psum(point_part, "tensor")
    center_part = times_block(point_vals.astype(jnp.bfloat16), kernel) / total_points
    back = rows_out(center_part)
    back_b_rows = rows_in(back.astype(jnp.bfloat16))
    third = back + cols_out(times_block(back_b_rows, upper)) + ridge_penalty * first
    weighted = scale_row * third
    image = weighted + rows_out(times_block_t(cols_in(weighted.astype(jnp.bfloat16)), lower))
    old_norm, curvature, cross, image_norm = lax.psum(
        (
            jnp.sum(residual * residual, axis=1, keepdims=True),
            jnp.sum(direction * image, axis=1, keepdims=True),
            jnp.sum(residual * image, axis=1, keepdims=True),
            jnp.sum(image * image, axis=1, keepdims=True),
        ),
        ("dp", "tensor"),
    )
    step_size = old_norm / curvature
    new_iterate = iterate + step_size * direction
    new_residual = residual - step_size * image
    new_norm = old_norm - 2.0 * step_size * cross + step_size * step_size * image_norm
    new_direction = new_residual + new_norm / old_norm * direction
    return (new_iterate, new_residual, new_direction)


def solution(mesh):
    nd, nt = mesh.shape["dp"], mesh.shape["tensor"]

    def local(points, centers, factors, *vectors):
        piece = vectors[-1].shape[1]
        pts = points.shape[0]
        vmem = 2 * (3 * piece * factors.shape[1] + nd * pts * piece)
        whole_tiles = piece % 128 == 0 and pts % (128 * nt) == 0 and pts <= piece
        if whole_tiles and nd % 2 == 0 and nd > SLOTS and vmem <= 42 * 1024 * 1024:
            return fused_shards(nd, nt, points, centers, factors, *vectors)
        return shards(points, centers, factors, *vectors)

    return jax.shard_map(
        local,
        mesh=mesh,
        in_specs=(
            P("dp", None),
            P(("dp", "tensor"), None),
            P("tensor", "dp"),
            P(("dp", "tensor")),
            P(None, ("dp", "tensor")),
            P(None, ("dp", "tensor")),
            P(None, ("dp", "tensor")),
        ),
        out_specs=(P(None, ("dp", "tensor")), P(None, ("dp", "tensor")), P(None, ("dp", "tensor"))),
        check_vma=False,
    )
```
